256 devices in a mesh: ctx: 32 (over y_hi, z, core), kvh: 8 (over y_lo, x).
Axes of the slice: x: 4, y: 4 (y_hi: 2, y_lo: 2; y = y_hi * 2 + y_lo), z: 8, core: 2. Of those that a mesh axis runs over, the one named last changes fastest.
Arguments:
- q_proj: bfloat16 [16384, 8192], P('ctx', 'kvh'), may hold values from -10 to 10
- key_projection: bfloat16 [16384, 1024], P('ctx', 'kvh'), may hold values from -10 to 10
- value_projection: bfloat16 [16384, 1024], P('ctx', 'kvh'), may hold values from -6 to 6
- doc_ids: int32 [16384], P(('ctx', 'kvh')), may hold values from 0 to 15, never falling along the last dimension, each value on 1 to 2048 neighbouring positions
Outputs:
- attended: bfloat16 [16384, 8192], P('ctx', 'kvh')
The draws below stay inside these ranges and needn't reach their ends.
Inputs may be any that keep to these rules, and one draw needn't show every extreme that they name: `doc_ids`: ids never fall along the sequence; every answer has 1 to 2048 tokens, one exactly that many.
All inputs are finite; a program needn't handle non-finite values.
Results may differ from the reference program's by a relative error of at most 0.011.
Values may be sent and summed in bfloat16 or wider, within the bound.
No kernel may reach another device: no remote copies, remote signals or barrier semaphores. Data moves between devices by JAX's collectives and lax.ppermute only.
A program may use at most 64 MiB of HBM per device.

```python
import math
import jax
import jax.numpy as jnp
import numpy as np
from jax import lax

HEAD_SIZE = 128
GROUP = 8
TOK_DEV = 512
KEY_VALUE_HEADS = 8
HQ = 64
PACKED_TOKENS = 16384
WINDOW = 2048
DOCS = 16
N_CTX = 32


def draw_q_proj(key, part):
    key = jax.random.fold_in(key, 11)
    rotary_base = jnp.clip(jax.random.normal(key, (PACKED_TOKENS, HQ, HEAD_SIZE), jnp.float32), -6.0, 6.0)
    return rotary_base.reshape(PACKED_TOKENS, HQ * HEAD_SIZE).astype(jnp.bfloat16)


def draw_key_projection(key, part):
    key = jax.random.fold_in(key, 13)
    rotary_base = jnp.clip(jax.random.normal(key, (PACKED_TOKENS, KEY_VALUE_HEADS, HEAD_SIZE), jnp.float32), -6.0, 6.0)
    return rotary_base.reshape(PACKED_TOKENS, KEY_VALUE_HEADS * HEAD_SIZE).astype(jnp.bfloat16)


def block_scale(stream_key, dims, pieces, low, top_value):
    def one(dim, shards_of):
        heights = jax.random.uniform(jax.random.fold_in(jax.random.fold_in(stream_key, 6), dim), (shards_of,), jnp.float32, low / len(pieces), top_value / len(pieces))
        return jnp.repeat(jnp.exp(heights), dims[dim] // shards_of).reshape((-1,) + (1,) * (len(dims) - dim - 1))

    level = one(*pieces[0])
    for cut in pieces[1:]:
        level = level * one(*cut)
    return level


def length_profile(number_of, total, bound, skew):
    loads = [(1 << 20) // math.isqrt(grade ** skew) + 1 for grade in range(2, number_of + 1)]
    surplus, counts = total - bound - (number_of - 1), [1] * (number_of - 1)
    while surplus > 0:
        candidates = [i for i in range(number_of - 1) if counts[i] < bound]
        mass, left = sum([loads[i] for i in candidates]), surplus
        for i in candidates:
            more = min(bound - counts[i], max(1, left * loads[i] // mass), surplus)
            counts[i] = counts[i] + more
            surplus = surplus - more
    return np.array([bound] + counts)


def ragged_sizes(own_key, count, total, bound, slope):
    if count == 2:
        one = jax.random.randint(own_key, (), max(1, total - bound), min(bound, total - 1) + 1)
        return jnp.stack([one, total - one])
    sizes = jnp.asarray(length_profile(count, total, bound, slope), jnp.int32)
    couples = (count - 1) // 2
    giver, sink = sizes[1:1 + 2 * couples:2], sizes[2:2 + 2 * couples:2]
    room = jnp.minimum(giver - 1, bound - sink)
    moved = jax.random.randint(jax.random.fold_in(own_key, 1), (couples,), 0, 1 << 20) % (room + 1)
    sizes = sizes.at[1:1 + 2 * couples:2].set(giver - moved).at[2:2 + 2 * couples:2].set(sink + moved)
    return sizes[jax.random.permutation(jax.random.fold_in(own_key, 2), count)]


def gaussian(rng, shape, scale, limit, shards=(), kind=jnp.bfloat16):
    level = block_scale(rng, shape, shards, -0.22, 0.18) if shards else 1.0
    entries = jax.random.normal(rng, shape, jnp.float32) * scale * level
    return jnp.minimum(jnp.maximum(entries, -limit), limit).astype(kind)


def setup_inputs(seed: int = 0) -> dict:
    arg_keys = jax.random.split(jax.random.key(seed), 5)
    return {
        "q_proj": draw_q_proj(jax.random.fold_in(arg_keys[4], 71), 0),
        "key_projection": draw_key_projection(jax.random.fold_in(arg_keys[4], 71), 0),
        "value_projection": gaussian(arg_keys[2], (PACKED_TOKENS, KEY_VALUE_HEADS * HEAD_SIZE), 1.0, 6.0, ((0, 32), (1, 8))),
        "doc_ids": jnp.searchsorted(jnp.cumsum(ragged_sizes(arg_keys[3], DOCS, PACKED_TOKENS, 4 * TOK_DEV, 2)), jnp.arange(PACKED_TOKENS), side="right").astype(jnp.int32),
    }


NEG = -1e+30
THETA = 1000000.0

def apply_rotary(x, token_positions):
    half = HEAD_SIZE // 2
    inv = THETA ** (-(2.0 * jnp.arange(half, dtype=jnp.float32)) / HEAD_SIZE)
    angle = token_positions.astype(jnp.float32)[:, None] * inv[None, :]
    cosine = jnp.cos(angle)[:, None, :]
    sine = jnp.sin(angle)[:, None, :]
    first = x[..., :half].astype(jnp.float32)
    second = x[..., half:].astype(jnp.float32)
    rotated = jnp.concatenate([first * cosine - second * sine, second * cosine + first * sine], axis=-1)
    return rotated.astype(jnp.bfloat16)

def reference(q_proj, key_projection, value_projection, doc_ids):
    token_positions = jnp.arange(PACKED_TOKENS, dtype=jnp.int32)
    queries = apply_rotary(q_proj.reshape(PACKED_TOKENS, HQ, HEAD_SIZE), token_positions)
    key_rows = apply_rotary(key_projection.reshape(PACKED_TOKENS, KEY_VALUE_HEADS, HEAD_SIZE), token_positions)
    value_rows = value_projection.reshape(PACKED_TOKENS, KEY_VALUE_HEADS, HEAD_SIZE)
    scale = 1.0 / jnp.sqrt(jnp.float32(HEAD_SIZE))

    def one_block(index):
        start = (index * TOK_DEV).astype(jnp.int32)
        qblock = lax.dynamic_slice_in_dim(queries, start, TOK_DEV, 0).astype(jnp.float32)
        qpos = start + jnp.arange(TOK_DEV, dtype=jnp.int32)
        qids = lax.dynamic_slice_in_dim(doc_ids, start, TOK_DEV, 0)
        running = jnp.full((HQ, TOK_DEV), NEG, jnp.float32)
        total = jnp.zeros((HQ, TOK_DEV), jnp.float32)
        acc = jnp.zeros((HQ, TOK_DEV, HEAD_SIZE), jnp.float32)
        for step in range(5):
            kstart = (start - step * TOK_DEV).astype(jnp.int32)
            kpos = kstart + jnp.arange(TOK_DEV, dtype=jnp.int32)
            safe = jnp.maximum(kstart, 0).astype(jnp.int32)
            kblock = lax.dynamic_slice_in_dim(key_rows, safe, TOK_DEV, 0)
            vblock = lax.dynamic_slice_in_dim(value_rows, safe, TOK_DEV, 0)
            kids = lax.dynamic_slice_in_dim(doc_ids, safe, TOK_DEV, 0)
            visible = (qids[:, None] == kids[None, :]) & (qpos[:, None] >= kpos[None, :])
            visible = visible & (qpos[:, None] - kpos[None, :] < WINDOW) & (kpos[None, :] >= 0)
            kwide = jnp.repeat(kblock, GROUP, axis=1).astype(jnp.float32)
            vwide = jnp.repeat(vblock, GROUP, axis=1).astype(jnp.float32)
            scores = jnp.einsum('thd,shd->hts', qblock, kwide) * scale
            scores = jnp.where(visible[None, :, :], scores, NEG)
            newmax = jnp.maximum(running, lax.optimization_barrier(jnp.max(scores, axis=-1)))
            factor = jnp.exp(running - newmax)
            weights = jnp.exp(scores - newmax[:, :, None])
            total = total * factor + lax.optimization_barrier(jnp.sum(weights, axis=-1))
            rounded = weights.astype(jnp.bfloat16).astype(jnp.float32)
            acc = acc * factor[:, :, None] + jnp.einsum('hts,shd->htd', rounded, vwide)
            running = newmax
        out = acc / total[:, :, None]
        return out.transpose(1, 0, 2).reshape(TOK_DEV, HQ * HEAD_SIZE).astype(jnp.bfloat16)
    blocks = lax.map(one_block, jnp.arange(N_CTX, dtype=jnp.int32))
    return blocks.reshape(PACKED_TOKENS, HQ * HEAD_SIZE)
```

```python
import functools

import jax
import jax.numpy as jnp
import numpy as np
from jax import lax
from jax.experimental import pallas as pl
from jax.experimental.pallas import tpu as pltpu
from jax.sharding import PartitionSpec as P

HEAD = 128
GROUP = 8
TOK = 512
N_CTX = 32
THETA = 1000000.0
NEG = -1e30
SCALE = float(np.log2(np.e) / np.sqrt(HEAD))
TQ = 128


def rotary_table():
    half = HEAD // 2
    inv = np.float32(THETA) ** (-(np.float32(2.0) * np.arange(half, dtype=np.float32)) / np.float32(HEAD))
    angle = np.arange(N_CTX * TOK, dtype=np.float32)[:, None] * inv.astype(np.float32)[None, :]
    wide = angle.astype(np.float64)
    table = np.concatenate([np.cos(wide), np.sin(wide)], axis=1).astype(np.float32)
    return table.reshape(N_CTX, TOK, HEAD)


def wide_factors(table):
    turned = pltpu.roll(table, HEAD // 2, 1)
    low = lax.broadcasted_iota(jnp.int32, table.shape, 1) < HEAD // 2
    return jnp.where(low, table, turned), jnp.where(low, -turned, table)


def rotate(x, cosine, sine):
    x = x.astype(jnp.float32)
    return (x * cosine + pltpu.roll(x, HEAD // 2, 1) * sine).astype(jnp.bfloat16)


def pack_kernel(ctx_ref, table_ref, k_ref, v_ref, out_ref):
    cosine, sine = wide_factors(table_ref[0])
    out_ref[:, :HEAD] = rotate(k_ref[...], cosine, sine)
    out_ref[:, HEAD:] = v_ref[...]


def twice(x):
    return jnp.concatenate([x, x], axis=1)


def prepare_block(kv_ref, kt, va, slot):
    kt[slot] = kv_ref[:, :HEAD].T
    va[slot, :, :HEAD] = kv_ref[:, HEAD:]
    va[slot, :, HEAD:] = jnp.ones((TOK, HEAD), jnp.bfloat16)


def far_tile(row, q, kt, va, slot, start, count, base, m_ref, acc_ref):
    rows = pl.ds(row, TQ)
    kpos = base + lax.broadcasted_iota(jnp.int32, (1, TOK), 1)
    key_bias = jnp.where(kpos >= start, 0.0, NEG)
    live = row + lax.broadcasted_iota(jnp.int32, (TQ, HEAD), 0) < count
    for h in range(GROUP):
        s = jnp.dot(q[h, rows, :], kt[slot], preferred_element_type=jnp.float32)
        s = s * SCALE + key_bias
        old = m_ref[h, rows, :]
        top = jnp.where(live, jnp.max(s, axis=1, keepdims=True), NEG)
        new = jnp.maximum(old, top)
        shift = jnp.where(live, new, -NEG)
        p = jnp.exp2(s - jnp.concatenate([shift] * (TOK // HEAD), axis=1))
        factor = jnp.exp2(old - new)
        m_ref[h, rows, :] = new
        update = jnp.dot(p.astype(jnp.bfloat16), va[slot], preferred_element_type=jnp.float32)
        acc_ref[h, rows, :] = acc_ref[h, rows, :] * twice(factor) + update


def far_blocks(bases, ctx_base, q, kt, va, start, count, m_ref, acc_ref):
    for slot, base in enumerate(bases):

        @pl.when((base < ctx_base) & (base + TOK > start))
        def _():
            def body(i, carry):
                far_tile(pl.multiple_of(i * TQ, TQ), q, kt, va, slot, start, count, base, m_ref, acc_ref)
                return carry

            lax.fori_loop(0, (count + TQ - 1) // TQ, body, 0)


def rotate_queries(q_ref, table_ref, q):
    cosine, sine = wide_factors(table_ref[0])
    for h in range(GROUP):
        q[h] = rotate(q_ref[:, h * HEAD : (h + 1) * HEAD], cosine, sine)


def document(ids, ids1, ids2, ctx):
    own = jnp.sum(ids[:8], axis=0, keepdims=True)
    first = own[:, :1]

    def matches(block):
        return jnp.sum(jnp.where(jnp.sum(block, axis=0, keepdims=True) == first, 1, 0))

    before = matches(ids[8:]) * lax.rem(ctx, 2)
    for other in (ids1, ids2):
        before = before + matches(other[:8]) + matches(other[8:])
    return own, ctx * TOK - before, matches(ids[:8])


def first_kernel(
    ctx_ref, table_ref, q_ref, own_ref, sib_ref, r1_ref, r1s_ref, ids_ref, ids1_ref, ids2_ref,
    m_out, acc_out, q, kt, va, bias,
):
    ctx = ctx_ref[0]
    other = ctx + 1 - 2 * lax.rem(ctx, 2)
    rotate_queries(q_ref, table_ref, q)
    own, start, count = document(ids_ref[...], ids1_ref[...], ids2_ref[...], ctx)
    for slot, ref in enumerate((own_ref, sib_ref, r1_ref, r1s_ref)):
        prepare_block(ref, kt, va, slot)
    column = jnp.broadcast_to(own, (HEAD, TOK)).T
    for t in range(TOK // TQ):
        rows = slice(t * TQ, (t + 1) * TQ)
        width = (t + 1) * TQ
        key = lax.broadcasted_iota(jnp.int32, (TQ, width), 1)
        query = t * TQ + lax.broadcasted_iota(jnp.int32, (TQ, width), 0)
        same = jnp.concatenate([column[rows]] * (width // HEAD), axis=1) == own[:, :width]
        bias[:, :width] = jnp.where(same & (key <= query), 0.0, NEG)
        for h in range(GROUP):
            s = jnp.dot(q[h, rows, :], kt[0, :, :width], preferred_element_type=jnp.float32)
            s = s * SCALE + bias[:, :width]
            top = jnp.broadcast_to(jnp.max(s, axis=1, keepdims=True), (TQ, HEAD))
            p = jnp.exp2(s - jnp.concatenate([top] * (width // HEAD), axis=1))
            m_out[h, rows, :] = top
            acc_out[h, rows, :] = jnp.dot(
                p.astype(jnp.bfloat16), va[0, :width, :], preferred_element_type=jnp.float32
            )
    bases = [other * TOK, (ctx - 2) * TOK, (other - 2) * TOK]
    far_blocks(bases, ctx * TOK, q, kt.at[1:], va.at[1:], start, count, m_out, acc_out)


def last_kernel(
    ctx_ref, table_ref, q_ref, r2_ref, r2s_ref, ids_ref, ids1_ref, ids2_ref, m_in, acc_in,
    out_ref, q, kt, va,
):
    ctx = ctx_ref[0]
    other = ctx + 1 - 2 * lax.rem(ctx, 2)
    _, start, count = document(ids_ref[...], ids1_ref[...], ids2_ref[...], ctx)
    bases = [(ctx - 4) * TOK, (other - 4) * TOK]

    @pl.when(start < jnp.maximum(bases[0], bases[1]) + TOK)
    def _():
        rotate_queries(q_ref, table_ref, q)
        for slot, ref in enumerate((r2_ref, r2s_ref)):
            prepare_block(ref, kt, va, slot)
        far_blocks(bases, ctx * TOK, q, kt, va, start, count, m_in, acc_in)

    for h in range(GROUP):
        acc = acc_in[h]
        out_ref[:, h * HEAD : (h + 1) * HEAD] = (acc[:, :HEAD] / acc[:, HEAD:]).astype(jnp.bfloat16)


def whole(shape):
    return pl.BlockSpec(shape, lambda i, ctx: (0,) * len(shape))


TABLE_SPEC = pl.BlockSpec((1, TOK, HEAD), lambda i, ctx: (ctx[0], 0, 0))
KV = (TOK, 2 * HEAD)
STATE = ((GROUP, TOK, HEAD), (GROUP, TOK, 2 * HEAD))
LIMIT = 48 * 2**20


def call(kernel, name, ins, outs, dtypes, scratch, flops):
    return pl.pallas_call(
        kernel,
        grid_spec=pltpu.PrefetchScalarGridSpec(
            num_scalar_prefetch=1,
            grid=(1,),
            in_specs=[TABLE_SPEC] + [whole(s) for s in ins],
            out_specs=[whole(s) for s in outs],
            scratch_shapes=scratch,
        ),
        out_shape=[jax.ShapeDtypeStruct(s, d) for s, d in zip(outs, dtypes)],
        compiler_params=pltpu.CompilerParams(vmem_limit_bytes=LIMIT),
        cost_estimate=pl.CostEstimate(flops=flops, bytes_accessed=2**21, transcendentals=0),
        name=name,
    )


def blocks_scratch(count):
    return [
        pltpu.VMEM((GROUP, TOK, HEAD), jnp.bfloat16),
        pltpu.VMEM((count, HEAD, TOK), jnp.bfloat16),
        pltpu.VMEM((count, TOK, 2 * HEAD), jnp.bfloat16),
    ]


def shifted(value, steps):
    return lax.ppermute(value, "ctx", [(i, i + steps) for i in range(N_CTX - steps)])


def swapped(value):
    return lax.ppermute(value, "ctx", [(i, i ^ 1) for i in range(N_CTX)])


def local(q_proj, key_projection, value_projection, doc_ids):
    table = jnp.asarray(rotary_table())
    index = lax.axis_index("ctx").astype(jnp.int32)
    ctx = index.reshape(1)
    place = lax.axis_index("kvh")
    spread = jnp.where(
        jnp.arange(TOK, dtype=jnp.int32) // doc_ids.shape[0] == place, jnp.tile(doc_ids, 8) + 1, 0
    ).astype(jnp.float32)
    ids = lax.all_to_all(jnp.broadcast_to(spread, (8, TOK)), "kvh", 0, 0, tiled=True)
    (own,) = call(pack_kernel, "pack", [(TOK, HEAD)] * 2, [KV], [jnp.bfloat16], [], 10**6)(
        ctx, table, key_projection, value_projection
    )
    sib = swapped(own)
    r1 = shifted(own, 2)
    r1s = swapped(r1)
    r2 = shifted(r1, 2)
    r2s = swapped(r2)
    both = jnp.concatenate([ids, swapped(ids)], axis=0)
    ids1 = shifted(both, 2)
    ids2 = shifted(both, 4)
    m, acc = call(
        first_kernel,
        "first",
        [(TOK, GROUP * HEAD)] + [KV] * 4 + [(16, TOK)] * 3,
        list(STATE),
        [jnp.float32] * 2,
        blocks_scratch(4) + [pltpu.VMEM((TQ, TOK), jnp.float32)],
        10**10,
    )(ctx, table, q_proj, own, sib, r1, r1s, both, ids1, ids2)
    (out,) = call(
        last_kernel,
        "last",
        [(TOK, GROUP * HEAD)] + [KV] * 2 + [(16, TOK)] * 3 + list(STATE),
        [(TOK, GROUP * HEAD)],
        [jnp.bfloat16],
        blocks_scratch(2),
        4 * 10**9,
    )(ctx, table, q_proj, r2, r2s, both, ids1, ids2, m, acc)
    return out


def solution(mesh):
    in_specs = (P("ctx", "kvh"), P("ctx", "kvh"), P("ctx", "kvh"), P(("ctx", "kvh")))
    return jax.shard_map(
        local, mesh=mesh, in_specs=in_specs, out_specs=P("ctx", "kvh"), check_vma=False
    )
```

```python
import functools

import jax
import jax.numpy as jnp
import numpy as np
from jax import lax
from jax.experimental import pallas as pl
from jax.experimental.pallas import tpu as pltpu
from jax.sharding import PartitionSpec as P

HEAD = 128
GROUP = 8
TOK = 512
N_CTX = 32
THETA = 1000000.0
NEG = -1e30
SCALE = float(np.log2(np.e) / np.sqrt(HEAD))
HALF = TOK // 2
ROWS = GROUP * HALF
KVH = 8
SPARE = 16


def rotary_table():
    half = HEAD // 2
    inv = np.float32(THETA) ** (-(np.float32(2.0) * np.arange(half, dtype=np.float32)) / np.float32(HEAD))
    angle = np.arange(N_CTX * TOK, dtype=np.float32)[:, None] * inv.astype(np.float32)[None, :]
    wide = angle.astype(np.float64)
    cosine, sine = np.cos(wide), np.sin(wide)
    table = np.concatenate([cosine, cosine, -sine, sine], axis=1).astype(np.float32)
    return table.reshape(N_CTX, TOK, 2 * HEAD)


def rotate(x, table):
    x = x.astype(jnp.float32)
    return (x * table[:, :HEAD] + pltpu.roll(x, HEAD // 2, 1) * table[:, HEAD:]).astype(jnp.bfloat16)


def pack_kernel(ctx_ref, ids, k, v, table_hbm, out, table, sem):
    copy = pltpu.make_async_copy(table_hbm.at[ctx_ref[0]], table, sem)
    copy.start()
    out[:TOK, HEAD:] = v[...]
    pieces, size = ids.shape
    wide = jnp.concatenate([ids[...], jnp.zeros((pieces, 2 * HEAD - size), jnp.float32)], axis=1)
    wide = jnp.concatenate([wide, jnp.zeros((SPARE - pieces, 2 * HEAD), jnp.float32)], axis=0)
    out[TOK:] = wide.astype(jnp.bfloat16)
    copy.wait()
    out[:TOK, :HEAD] = rotate(k[...], table)


def twice(x):
    return jnp.concatenate([x, x], axis=-1)


def widened(x, width):
    return jnp.concatenate([x] * (width // HEAD), axis=-1)


def pieces_of(message):
    return message[TOK:].astype(jnp.float32)


def id_row(parts):
    size = TOK // KVH
    parts = parts[:KVH]
    lane = lax.broadcasted_iota(jnp.int32, (2 * HEAD, TOK), 1)
    place = (lax.rem(lane, size) == lax.broadcasted_iota(jnp.int32, (2 * HEAD, TOK), 0)).astype(jnp.float32)
    spread = jnp.dot(parts, place, preferred_element_type=jnp.float32)
    mine = lax.broadcasted_iota(jnp.int32, (KVH, TOK), 1) // size
    mine = mine == lax.broadcasted_iota(jnp.int32, (KVH, TOK), 0)
    return jnp.sum(jnp.where(mine, spread, 0.0), axis=0, keepdims=True)


def matches(block, first):
    return jnp.sum(jnp.where(block == first, 1, 0))


def prepare_block(kv, kt, va):
    kt[...] = kv[:TOK, :HEAD].T
    va[:, :HEAD] = kv[:TOK, HEAD:]
    va[:, HEAD:] = jnp.ones((TOK, HEAD), jnp.bfloat16)


def own_half(half, queries, kt, va, column, row, m, acc):
    width = (half + 1) * HALF
    rows = slice(half * HALF, width)
    key = lax.broadcasted_iota(jnp.int32, (HALF, width), 1)
    query = half * HALF + lax.broadcasted_iota(jnp.int32, (HALF, width), 0)
    same = widened(column[rows], width) == row[:, :width]
    bias = jnp.where(same & (key <= query), 0.0, NEG)
    s = jnp.dot(queries[half], kt[:, :width], preferred_element_type=jnp.float32)
    s = s.reshape(GROUP, HALF, width) * SCALE + bias[None]
    top = jnp.broadcast_to(jnp.max(s, axis=2, keepdims=True), (GROUP, HALF, HEAD))
    p = jnp.exp2(s - widened(top, width)).reshape(ROWS, width).astype(jnp.bfloat16)
    m[half] = top.reshape(ROWS, HEAD)
    acc[half] = jnp.dot(p, va[:width], preferred_element_type=jnp.float32)


def far_half(half, queries, kt, va, base, start, count, m, acc):
    kpos = base + lax.broadcasted_iota(jnp.int32, (1, TOK), 1)
    key_bias = jnp.where(kpos >= start, 0.0, NEG)
    live = half * HALF + lax.broadcasted_iota(jnp.int32, (HALF, HEAD), 0) < count
    s = jnp.dot(queries[half], kt[...], preferred_element_type=jnp.float32)
    s = (s * SCALE + key_bias).reshape(GROUP, HALF, TOK)
    old = m[half].reshape(GROUP, HALF, HEAD)
    top = jnp.where(live[None], jnp.max(s, axis=2, keepdims=True), NEG)
    new = jnp.maximum(old, top)
    shift = jnp.where(live[None], new, -NEG)
    p = jnp.exp2(s - widened(shift, TOK)).reshape(ROWS, TOK).astype(jnp.bfloat16)
    factor = jnp.exp2(old - new).reshape(ROWS, HEAD)
    m[half] = new.reshape(ROWS, HEAD)
    update = jnp.dot(p, va[...], preferred_element_type=jnp.float32)
    acc[half] = acc[half] * twice(factor) + update


def far_blocks(bases, messages, ctx_base, queries, kt, va, start, count, m, acc):
    def seen(base):
        return (base < ctx_base) & (base + TOK > start)

    for slot, (base, message) in enumerate(zip(bases, messages)):

        @pl.when(seen(base))
        def _():
            prepare_block(message, kt.at[slot], va.at[slot])

    def visit(slot, carry):
        base = bases[0]
        for i in range(1, len(bases)):
            base = jnp.where(slot == i, bases[i], base)

        @pl.when(seen(base))
        def _():
            def body(half, inner):
                far_half(half, queries, kt.at[slot], va.at[slot], base, start, count, m, acc)
                return inner

            lax.fori_loop(0, (count + HALF - 1) // HALF, body, 0)

        return carry

    lax.fori_loop(0, len(bases), visit, 0)


def finish(acc, out):
    for half in range(2):
        for h in range(GROUP):
            a = acc[half, h * HALF : (h + 1) * HALF]
            out[half * HALF : (half + 1) * HALF, h * HEAD : (h + 1) * HEAD] = (
                a[:, :HEAD] / a[:, HEAD:]
            ).astype(jnp.bfloat16)


def own_kernel(ctx_ref, own, table_hbm, q_hbm, queries, m, acc, table, raw, kt, va, sems):
    copies = [
        pltpu.make_async_copy(table_hbm.at[ctx_ref[0]], table, sems.at[0]),
        pltpu.make_async_copy(q_hbm, raw, sems.at[1]),
    ]
    for copy in copies:
        copy.start()
    row = id_row(pieces_of(own))
    column = jnp.broadcast_to(row, (HEAD, TOK)).T
    prepare_block(own, kt, va)
    for copy in copies:
        copy.wait()
    for h in range(GROUP):
        turned = rotate(raw[:, h * HEAD : (h + 1) * HEAD], table)
        for half in range(2):
            queries[half, h * HALF : (h + 1) * HALF] = turned[half * HALF : (half + 1) * HALF]
    for half in range(2):
        own_half(half, queries, kt, va, column, row, m, acc)


def near_start(ctx, own, sib, r1, r1s):
    mine = pieces_of(own)
    first = mine[:1, :1]
    before = matches(pieces_of(sib), first) * lax.rem(ctx, 2)
    before = before + matches(pieces_of(r1), first) + matches(pieces_of(r1s), first)
    return ctx * TOK - before, matches(mine, first), first


def chip_before(ctx):
    return (ctx - 2 - lax.rem(ctx, 2)) * TOK


def near_kernel(ctx_ref, own, sib, r1, r1s, queries, m_in, acc_in, out_hbm, m, acc, kt, va, out, sem):
    ctx = ctx_ref[0]
    other = ctx + 1 - 2 * lax.rem(ctx, 2)
    start, count, _ = near_start(ctx, own, sib, r1, r1s)
    bases = [other * TOK, (ctx - 2) * TOK, (other - 2) * TOK]
    far_blocks(bases, [sib, r1, r1s], ctx * TOK, queries, kt, va, start, count, m, acc)
    finish(acc, out)
    send = pltpu.make_async_copy(out, out_hbm, sem)
    send.start()
    send.wait()


def last_kernel(
    ctx_ref, own, sib, r1, r1s, r2, r2s, queries, m_in, acc_in, done_hbm,
    out_hbm, m, acc, kt, va, out, sem,
):
    ctx = ctx_ref[0]
    other = ctx + 1 - 2 * lax.rem(ctx, 2)
    near, count, first = near_start(ctx, own, sib, r1, r1s)

    @pl.when((near <= chip_before(ctx)) & (ctx >= 4))
    def _():
        start = near - matches(pieces_of(r2), first) - matches(pieces_of(r2s), first)

        @pl.when(start < near)
        def _():
            bases = [(ctx - 4) * TOK, (other - 4) * TOK]
            far_blocks(bases, [r2, r2s], ctx * TOK, queries, kt, va, start, count, m, acc)
            finish(acc, out)
            send = pltpu.make_async_copy(out, out_hbm, sem)
            send.start()
            send.wait()


IN_SMEM = pl.BlockSpec(memory_space=pltpu.SMEM)
IN_VMEM = pl.BlockSpec(memory_space=pltpu.VMEM)
IN_HBM = pl.BlockSpec(memory_space=pltpu.HBM)
MESSAGE = jax.ShapeDtypeStruct((TOK + SPARE, 2 * HEAD), jnp.bfloat16)
OUT = jax.ShapeDtypeStruct((TOK, GROUP * HEAD), jnp.bfloat16)
QUERIES = jax.ShapeDtypeStruct((2, ROWS, HEAD), jnp.bfloat16)
TOP = jax.ShapeDtypeStruct((2, ROWS, HEAD), jnp.float32)
ACC = jax.ShapeDtypeStruct((2, ROWS, 2 * HEAD), jnp.float32)
TABLE = pltpu.VMEM((TOK, 2 * HEAD), jnp.float32)
LIMIT = 44 * 2**20


def like(t):
    return pltpu.VMEM(t.shape, t.dtype)


def blocks(count):
    lead = (count,) if count else ()
    return [pltpu.VMEM(lead + (HEAD, TOK), jnp.bfloat16), pltpu.VMEM(lead + (TOK, 2 * HEAD), jnp.bfloat16)]


def call(kernel, name, ins, outs, scratch, flops, **more):
    specs, types = zip(*outs)
    return pl.pallas_call(
        kernel,
        in_specs=[IN_SMEM] + ins,
        out_specs=list(specs),
        out_shape=list(types),
        scratch_shapes=scratch,
        compiler_params=pltpu.CompilerParams(vmem_limit_bytes=LIMIT),
        cost_estimate=pl.CostEstimate(flops=flops, bytes_accessed=2**21, transcendentals=0),
        name=name,
        **more,
    )


def shifted(value, steps):
    return lax.ppermute(value, "ctx", [(i, i + steps) for i in range(N_CTX - steps)])


def swapped(value):
    return lax.ppermute(value, "ctx", [(i, i ^ 1) for i in range(N_CTX)])


def local(q_proj, key_projection, value_projection, doc_ids):
    table = jnp.asarray(rotary_table())
    ctx = lax.axis_index("ctx").astype(jnp.int32).reshape(1)
    mine = jnp.broadcast_to((doc_ids + 1).astype(jnp.float32), (KVH, doc_ids.shape[0]))
    ids = lax.all_to_all(mine, "kvh", 0, 0, tiled=True)
    dma = pltpu.SemaphoreType.DMA
    (own,) = call(
        pack_kernel, "pack", [IN_VMEM] * 3 + [IN_HBM], [(IN_VMEM, MESSAGE)], [TABLE, dma], 10**6
    )(ctx, ids, key_projection, value_projection, table)
    r1 = shifted(own, 2)
    sib = swapped(own)
    queries, m, acc = call(
        own_kernel,
        "own",
        [IN_VMEM] + [IN_HBM] * 2,
        [(IN_VMEM, QUERIES), (IN_VMEM, TOP), (IN_VMEM, ACC)],
        [TABLE, like(OUT)] + blocks(0) + [dma((2,))],
        3 * 10**9,
    )(ctx, own, table, q_proj)
    r1, queries = lax.optimization_barrier((r1, queries))
    r2 = shifted(r1, 2)
    r1s = swapped(r1)
    out, m, acc = call(
        near_kernel,
        "near",
        [IN_VMEM] * 7,
        [(IN_HBM, OUT), (IN_VMEM, TOP), (IN_VMEM, ACC)],
        blocks(3) + [like(OUT), dma],
        8 * 10**9,
        input_output_aliases={6: 1, 7: 2},
    )(ctx, own, sib, r1, r1s, queries, m, acc)
    r2, m = lax.optimization_barrier((r2, m))
    r2s = swapped(r2)
    out, _, _ = call(
        last_kernel,
        "last",
        [IN_VMEM] * 9 + [IN_HBM],
        [(IN_HBM, OUT), (IN_VMEM, TOP), (IN_VMEM, ACC)],
        blocks(2) + [like(OUT), dma],
        10**9,
        input_output_aliases={8: 1, 9: 2, 10: 0},
    )(ctx, own, sib, r1, r1s, r2, r2s, queries, m, acc, out)
    return out


def solution(mesh):
    in_specs = (P("ctx", "kvh"), P("ctx", "kvh"), P("ctx", "kvh"), P(("ctx", "kvh")))
    return jax.shard_map(
        local, mesh=mesh, in_specs=in_specs, out_specs=P("ctx", "kvh"), check_vma=False
    )
```

```python
import functools

import jax
import jax.numpy as jnp
import numpy as np
from jax import lax
from jax.experimental import pallas as pl
from jax.experimental.pallas import tpu as pltpu
from jax.sharding import PartitionSpec as P

HEAD = 128
GROUP = 8
TOK = 512
N_CTX = 32
THETA = 1000000.0
NEG = -1e30
SCALE = float(np.log2(np.e) / np.sqrt(HEAD))
HALF = TOK // 2
ROWS = GROUP * HALF
KVH = 8
SPARE = 16


def rotary_table():
    half = HEAD // 2
    inv = np.float32(THETA) ** (-(np.float32(2.0) * np.arange(half, dtype=np.float32)) / np.float32(HEAD))
    angle = np.arange(N_CTX * TOK, dtype=np.float32)[:, None] * inv.astype(np.float32)[None, :]
    wide = angle.astype(np.float64)
    cosine, sine = np.cos(wide), np.sin(wide)
    table = np.concatenate([cosine, cosine, -sine, sine], axis=1).astype(np.float32)
    return table.reshape(N_CTX, TOK, 2 * HEAD)


def rotate(x, table):
    x = x.astype(jnp.float32)
    return (x * table[:, :HEAD] + pltpu.roll(x, HEAD // 2, 1) * table[:, HEAD:]).astype(jnp.bfloat16)


def message_kernel(ctx_ref, k_hbm, v_hbm, table_hbm, out, k, v, table, sems):
    copies = [
        pltpu.make_async_copy(table_hbm.at[ctx_ref[0]], table, sems.at[0]),
        pltpu.make_async_copy(k_hbm, k, sems.at[1]),
        pltpu.make_async_copy(v_hbm, v, sems.at[2]),
    ]
    for copy in copies:
        copy.start()
    out[TOK:] = jnp.zeros((SPARE, 2 * HEAD), jnp.bfloat16)
    for copy in copies:
        copy.wait()
    out[:TOK, HEAD:] = v[...]
    out[:TOK, :HEAD] = rotate(k[...], table)


def ids_kernel(ids, message_in, message):
    pieces, size = ids.shape
    wide = jnp.concatenate([ids[...], jnp.zeros((pieces, 2 * HEAD - size), jnp.float32)], axis=1)
    wide = jnp.concatenate([wide, jnp.zeros((SPARE - pieces, 2 * HEAD), jnp.float32)], axis=0)
    message[TOK:] = wide.astype(jnp.bfloat16)


def queries_kernel(ctx_ref, q_hbm, table_hbm, queries, raw, table, sems):
    copies = [
        pltpu.make_async_copy(table_hbm.at[ctx_ref[0]], table, sems.at[0]),
        pltpu.make_async_copy(q_hbm, raw, sems.at[1]),
    ]
    for copy in copies:
        copy.start()
    for copy in copies:
        copy.wait()
    for h in range(GROUP):
        turned = rotate(raw[:, h * HEAD : (h + 1) * HEAD], table)
        for half in range(2):
            queries[half, h * HALF : (h + 1) * HALF] = turned[half * HALF : (half + 1) * HALF]


def twice(x):
    return jnp.concatenate([x, x], axis=-1)


def widened(x, width):
    return jnp.concatenate([x] * (width // HEAD), axis=-1)


def pieces_of(message):
    return message[TOK:].astype(jnp.float32)


def id_row(parts):
    size = TOK // KVH
    parts = parts[:KVH]
    lane = lax.broadcasted_iota(jnp.int32, (2 * HEAD, TOK), 1)
    place = (lax.rem(lane, size) == lax.broadcasted_iota(jnp.int32, (2 * HEAD, TOK), 0)).astype(jnp.float32)
    spread = jnp.dot(parts, place, preferred_element_type=jnp.float32)
    mine = lax.broadcasted_iota(jnp.int32, (KVH, TOK), 1) // size
    mine = mine == lax.broadcasted_iota(jnp.int32, (KVH, TOK), 0)
    return jnp.sum(jnp.where(mine, spread, 0.0), axis=0, keepdims=True)


def matches(block, first):
    return jnp.sum(jnp.where(block == first, 1, 0))


def prepare_block(kv, kt, va):
    kt[...] = kv[:TOK, :HEAD].T
    va[:, :HEAD] = kv[:TOK, HEAD:]
    va[:, HEAD:] = jnp.ones((TOK, HEAD), jnp.bfloat16)


def own_half(half, queries, kt, va, column, row, m, acc):
    width = (half + 1) * HALF
    rows = slice(half * HALF, width)
    key = lax.broadcasted_iota(jnp.int32, (HALF, width), 1)
    query = half * HALF + lax.broadcasted_iota(jnp.int32, (HALF, width), 0)
    same = widened(column[rows], width) == row[:, :width]
    bias = jnp.where(same & (key <= query), 0.0, NEG)
    s = jnp.dot(queries[half], kt[:, :width], preferred_element_type=jnp.float32)
    s = s.reshape(GROUP, HALF, width) * SCALE + bias[None]
    top = jnp.broadcast_to(jnp.max(s, axis=2, keepdims=True), (GROUP, HALF, HEAD))
    p = jnp.exp2(s - widened(top, width)).reshape(ROWS, width).astype(jnp.bfloat16)
    m[half] = top.reshape(ROWS, HEAD)
    acc[half] = jnp.dot(p, va[:width], preferred_element_type=jnp.float32)


def whole_half(half, queries, kt, va, m, acc):
    s = jnp.dot(queries[half], kt[...], preferred_element_type=jnp.float32) * SCALE
    old = m[half]
    new = jnp.maximum(old, jnp.max(s, axis=1, keepdims=True))
    p = jnp.exp2(s - widened(new, TOK)).astype(jnp.bfloat16)
    m[half] = new
    update = jnp.dot(p, va[...], preferred_element_type=jnp.float32)
    acc[half] = acc[half] * twice(jnp.exp2(old - new)) + update


def part_half(half, skip, queries, kt, va, base, start, count, m, acc):
    width = TOK - skip
    kpos = base + skip + lax.broadcasted_iota(jnp.int32, (1, width), 1)
    key_bias = jnp.where(kpos >= start, 0.0, NEG)
    live = half * HALF + lax.broadcasted_iota(jnp.int32, (HALF, HEAD), 0) < count
    s = jnp.dot(queries[half], kt[:, skip:], preferred_element_type=jnp.float32)
    s = (s * SCALE + key_bias).reshape(GROUP, HALF, width)
    old = m[half].reshape(GROUP, HALF, HEAD)
    top = jnp.where(live[None], jnp.max(s, axis=2, keepdims=True), NEG)
    new = jnp.maximum(old, top)
    shift = jnp.where(live[None], new, -NEG)
    p = jnp.exp2(s - widened(shift, width)).reshape(ROWS, width).astype(jnp.bfloat16)
    factor = jnp.exp2(old - new).reshape(ROWS, HEAD)
    m[half] = new.reshape(ROWS, HEAD)
    update = jnp.dot(p, va[skip:], preferred_element_type=jnp.float32)
    acc[half] = acc[half] * twice(factor) + update


def far_block(base, message, wanted, queries, kt, va, start, count, m, acc):
    @pl.when(wanted & (base + TOK > start))
    def _():
        prepare_block(message, kt, va)

        def body(half, carry):
            whole = (start <= base) & (count >= (half + 1) * HALF)
            short = start >= base + HALF

            @pl.when(whole)
            def _():
                whole_half(half, queries, kt, va, m, acc)

            @pl.when(jnp.logical_not(whole | short))
            def _():
                part_half(half, 0, queries, kt, va, base, start, count, m, acc)

            @pl.when(short)
            def _():
                part_half(half, HALF, queries, kt, va, base, start, count, m, acc)

            return carry

        lax.fori_loop(0, (count + HALF - 1) // HALF, body, 0)


def finish(half, acc, out):
    for h in range(GROUP):
        a = acc[half, h * HALF : (h + 1) * HALF]
        out[half * HALF : (half + 1) * HALF, h * HEAD : (h + 1) * HEAD] = (
            a[:, :HEAD] / a[:, HEAD:]
        ).astype(jnp.bfloat16)


def own_kernel(own, queries, m, acc, kt, va):
    row = id_row(pieces_of(own))
    column = jnp.broadcast_to(row, (HEAD, TOK)).T
    prepare_block(own, kt, va)
    for half in range(2):
        own_half(half, queries, kt, va, column, row, m, acc)


def near_start(ctx, own, sib, r1, r1s):
    mine = pieces_of(own)
    first = mine[:1, :1]
    before = matches(pieces_of(sib), first) * lax.rem(ctx, 2)
    before = before + matches(pieces_of(r1), first) + matches(pieces_of(r1s), first)
    return ctx * TOK - before, matches(mine, first), first


def near_kernel(ctx_ref, own, sib, r1, r1s, queries, m_in, acc_in, m, acc, kt, va):
    ctx = ctx_ref[0]
    odd = lax.rem(ctx, 2) == 1
    start, count, _ = near_start(ctx, own, sib, r1, r1s)
    state = (queries, kt, va, start, count, m, acc)
    far_block((ctx - 1) * TOK, sib, odd, *state)
    far_block((ctx - 1) * TOK, r1s, jnp.logical_not(odd), *state)
    far_block((ctx - 2) * TOK, r1, ctx >= 2, *state)


def last_kernel(
    ctx_ref, own, sib, r1, r1s, r2, r2s, queries, m_in, acc_in, out_hbm, m, acc, kt, va, out, sems
):
    ctx = ctx_ref[0]
    odd = lax.rem(ctx, 2) == 1
    near, count, first = near_start(ctx, own, sib, r1, r1s)
    before = matches(pieces_of(r2), first) + matches(pieces_of(r2s), first)
    start = near - before
    state = (queries, kt, va, start, count, m, acc)
    far_block((ctx - 3) * TOK, r1s, odd & (ctx >= 3), *state)
    far_block((ctx - 3) * TOK, r2s, jnp.logical_not(odd) & (ctx >= 3), *state)
    far_block((ctx - 4) * TOK, r2, ctx >= 4, *state)
    sends = []
    for half in range(2):
        finish(half, acc, out)
        rows = pl.ds(half * HALF, HALF)
        sends.append(pltpu.make_async_copy(out.at[rows], out_hbm.at[rows], sems.at[half]))
        sends[-1].start()
    for send in sends:
        send.wait()


IN_SMEM = pl.BlockSpec(memory_space=pltpu.SMEM)
IN_VMEM = pl.BlockSpec(memory_space=pltpu.VMEM)
IN_HBM = pl.BlockSpec(memory_space=pltpu.HBM)
MESSAGE = jax.ShapeDtypeStruct((TOK + SPARE, 2 * HEAD), jnp.bfloat16)
OUT = jax.ShapeDtypeStruct((TOK, GROUP * HEAD), jnp.bfloat16)
QUERIES = jax.ShapeDtypeStruct((2, ROWS, HEAD), jnp.bfloat16)
TOP = jax.ShapeDtypeStruct((2, ROWS, HEAD), jnp.float32)
ACC = jax.ShapeDtypeStruct((2, ROWS, 2 * HEAD), jnp.float32)
TABLE = pltpu.VMEM((TOK, 2 * HEAD), jnp.float32)
LIMIT = 44 * 2**20


def like(t):
    return pltpu.VMEM(t.shape, t.dtype)


BLOCK = [pltpu.VMEM((HEAD, TOK), jnp.bfloat16), pltpu.VMEM((TOK, 2 * HEAD), jnp.bfloat16)]


def call(kernel, name, ins, outs, scratch, flops, **more):
    specs, types = zip(*outs)
    return pl.pallas_call(
        kernel,
        in_specs=ins,
        out_specs=list(specs),
        out_shape=list(types),
        scratch_shapes=scratch,
        compiler_params=pltpu.CompilerParams(vmem_limit_bytes=LIMIT),
        cost_estimate=pl.CostEstimate(flops=flops, bytes_accessed=2**21, transcendentals=0),
        name=name,
        **more,
    )


def shifted(value, steps):
    return lax.ppermute(value, "ctx", [(i, i + steps) for i in range(N_CTX - steps)])


def swapped(value, senders=(0, 1)):
    return lax.ppermute(value, "ctx", [(i, i ^ 1) for i in range(N_CTX) if i % 2 in senders])


def local(q_proj, key_projection, value_projection, doc_ids):
    table = jnp.asarray(rotary_table())
    ctx = lax.axis_index("ctx").astype(jnp.int32).reshape(1)
    mine = jnp.broadcast_to((doc_ids + 1).astype(jnp.float32), (KVH, doc_ids.shape[0]))
    ids = lax.all_to_all(mine, "kvh", 0, 0, tiled=True)
    dma = pltpu.SemaphoreType.DMA
    rows = pltpu.VMEM((TOK, HEAD), jnp.bfloat16)
    (message,) = call(
        message_kernel,
        "message",
        [IN_SMEM] + [IN_HBM] * 3,
        [(IN_VMEM, MESSAGE)],
        [rows, rows, TABLE, dma((3,))],
        2 * 10**9,
    )(ctx, key_projection, value_projection, table)
    (queries,) = call(
        queries_kernel,
        "queries",
        [IN_SMEM] + [IN_HBM] * 2,
        [(IN_VMEM, QUERIES)],
        [like(OUT), TABLE, dma((2,))],
        2 * 10**9,
    )(ctx, q_proj, table)
    (own,) = call(
        ids_kernel, "ids", [IN_VMEM] * 2, [(IN_VMEM, MESSAGE)], [], 10**6, input_output_aliases={1: 0}
    )(ids, message)
    r1 = shifted(own, 2)
    sib = swapped(own, (0,))
    m, acc = call(
        own_kernel, "own", [IN_VMEM] * 2, [(IN_VMEM, TOP), (IN_VMEM, ACC)], BLOCK, 3 * 10**9
    )(own, queries)
    r1, m = lax.optimization_barrier((r1, m))
    r2 = shifted(r1, 2)
    r1s = swapped(r1)
    m, acc = call(
        near_kernel,
        "near",
        [IN_SMEM] + [IN_VMEM] * 7,
        [(IN_VMEM, TOP), (IN_VMEM, ACC)],
        BLOCK,
        6 * 10**9,
        input_output_aliases={6: 0, 7: 1},
    )(ctx, own, sib, r1, r1s, queries, m, acc)
    r2, m = lax.optimization_barrier((r2, m))
    r2s = swapped(r2, (1,))
    out, _, _ = call(
        last_kernel,
        "last",
        [IN_SMEM] + [IN_VMEM] * 9,
        [(IN_HBM, OUT), (IN_VMEM, TOP), (IN_VMEM, ACC)],
        BLOCK + [like(OUT), dma((2,))],
        6 * 10**9,
        input_output_aliases={8: 1, 9: 2},
    )(ctx, own, sib, r1, r1s, r2, r2s, queries, m, acc)
    return out


def solution(mesh):
    in_specs = (P("ctx", "kvh"), P("ctx", "kvh"), P("ctx", "kvh"), P(("ctx", "kvh")))
    return jax.shard_map(
        local, mesh=mesh, in_specs=in_specs, out_specs=P("ctx", "kvh"), check_vma=False
    )
```

```python
import functools

import jax
import jax.numpy as jnp
import numpy as np
from jax import lax
from jax.experimental import pallas as pl
from jax.experimental.pallas import tpu as pltpu
from jax.sharding import PartitionSpec as P

HEAD = 128
GROUP = 8
TOK = 512
N_CTX = 32
THETA = 1000000.0
NEG = -1e30
SCALE = float(np.log2(np.e) / np.sqrt(HEAD))
HALF = TOK // 2
ROWS = GROUP * HALF
KVH = 8
SPARE = 16


def rotary_table():
    half = HEAD // 2
    inv = np.float32(THETA) ** (-(np.float32(2.0) * np.arange(half, dtype=np.float32)) / np.float32(HEAD))
    angle = np.arange(N_CTX * TOK, dtype=np.float32)[:, None] * inv.astype(np.float32)[None, :]
    wide = angle.astype(np.float64)
    cosine, sine = np.cos(wide), np.sin(wide)
    table = np.concatenate([cosine, cosine, -sine, sine], axis=1).astype(np.float32)
    return table.reshape(N_CTX, TOK, 2 * HEAD)


def rotate(x, table):
    x = x.astype(jnp.float32)
    return (x * table[:, :HEAD] + pltpu.roll(x, HEAD // 2, 1) * table[:, HEAD:]).astype(jnp.bfloat16)


def spread_kernel(ids, out):
    out[...] = jnp.broadcast_to(ids[...] + 1, out.shape).astype(jnp.float32)


def message_kernel(ctx_ref, k_hbm, v_hbm, table_hbm, out, same, k, v, table, sems):
    copies = [
        pltpu.make_async_copy(table_hbm.at[ctx_ref[0]], table, sems.at[0]),
        pltpu.make_async_copy(k_hbm, k, sems.at[1]),
        pltpu.make_async_copy(v_hbm, v, sems.at[2]),
    ]
    for copy in copies:
        copy.start()
    out[TOK:] = jnp.zeros((SPARE, 2 * HEAD), jnp.bfloat16)
    for copy in copies:
        copy.wait()
    turned = rotate(k[...], table)
    for target in (out, same):
        target[:TOK, HEAD:] = v[...]
        target[:TOK, :HEAD] = turned


def ids_kernel(ids, message_in, message):
    pieces, size = ids.shape
    wide = jnp.concatenate([ids[...], jnp.zeros((pieces, 2 * HEAD - size), jnp.float32)], axis=1)
    wide = jnp.concatenate([wide, jnp.zeros((SPARE - pieces, 2 * HEAD), jnp.float32)], axis=0)
    message[TOK:] = wide.astype(jnp.bfloat16)


def queries_kernel(ctx_ref, q_hbm, table_hbm, queries, raw, table, sems):
    copies = [
        pltpu.make_async_copy(table_hbm.at[ctx_ref[0]], table, sems.at[0]),
        pltpu.make_async_copy(q_hbm, raw, sems.at[1]),
    ]
    for copy in copies:
        copy.start()
    for copy in copies:
        copy.wait()
    for h in range(GROUP):
        turned = rotate(raw[:, h * HEAD : (h + 1) * HEAD], table)
        for half in range(2):
            queries[half, h * HALF : (h + 1) * HALF] = turned[half * HALF : (half + 1) * HALF]


def twice(x):
    return jnp.concatenate([x, x], axis=-1)


def widened(x, width):
    return jnp.concatenate([x] * (width // HEAD), axis=-1)


def pieces_of(message):
    return message[TOK:].astype(jnp.float32)


def id_row(parts):
    size = TOK // KVH
    parts = parts[:KVH]
    lane = lax.broadcasted_iota(jnp.int32, (2 * HEAD, TOK), 1)
    place = (lax.rem(lane, size) == lax.broadcasted_iota(jnp.int32, (2 * HEAD, TOK), 0)).astype(jnp.float32)
    spread = jnp.dot(parts, place, preferred_element_type=jnp.float32)
    mine = lax.broadcasted_iota(jnp.int32, (KVH, TOK), 1) // size
    mine = mine == lax.broadcasted_iota(jnp.int32, (KVH, TOK), 0)
    return jnp.sum(jnp.where(mine, spread, 0.0), axis=0, keepdims=True)


def matches(block, first):
    return jnp.sum(jnp.where(block == first, 1, 0))


def prepare_block(kv, kt, va):
    kt[...] = kv[:TOK, :HEAD].T
    va[:, :HEAD] = kv[:TOK, HEAD:]
    va[:, HEAD:] = jnp.ones((TOK, HEAD), jnp.bfloat16)


def own_half(half, queries, kt, va, column, row, m, acc):
    width = (half + 1) * HALF
    rows = slice(half * HALF, width)
    key = lax.broadcasted_iota(jnp.int32, (HALF, width), 1)
    query = half * HALF + lax.broadcasted_iota(jnp.int32, (HALF, width), 0)
    same = widened(column[rows], width) == row[:, :width]
    bias = jnp.where(same & (key <= query), 0.0, NEG)
    s = jnp.dot(queries[half], kt[:, :width], preferred_element_type=jnp.float32)
    s = s.reshape(GROUP, HALF, width) * SCALE + bias[None]
    top = jnp.broadcast_to(jnp.max(s, axis=2, keepdims=True), (GROUP, HALF, HEAD))
    p = jnp.exp2(s - widened(top, width)).reshape(ROWS, width).astype(jnp.bfloat16)
    m[half] = top.reshape(ROWS, HEAD)
    acc[half] = jnp.dot(p, va[:width], preferred_element_type=jnp.float32)


def whole_half(half, queries, kt, va, m, acc):
    s = jnp.dot(queries[half], kt[...], preferred_element_type=jnp.float32) * SCALE
    old = m[half]
    new = jnp.maximum(old, jnp.max(s, axis=1, keepdims=True))
    p = jnp.exp2(s - widened(new, TOK)).astype(jnp.bfloat16)
    m[half] = new
    update = jnp.dot(p, va[...], preferred_element_type=jnp.float32)
    acc[half] = acc[half] * twice(jnp.exp2(old - new)) + update


def part_half(half, skip, queries, kt, va, base, start, count, m, acc):
    width = TOK - skip
    kpos = base + skip + lax.broadcasted_iota(jnp.int32, (1, width), 1)
    key_bias = jnp.where(kpos >= start, 0.0, NEG)
    live = half * HALF + lax.broadcasted_iota(jnp.int32, (HALF, HEAD), 0) < count
    s = jnp.dot(queries[half], kt[:, skip:], preferred_element_type=jnp.float32)
    s = (s * SCALE + key_bias).reshape(GROUP, HALF, width)
    old = m[half].reshape(GROUP, HALF, HEAD)
    top = jnp.where(live[None], jnp.max(s, axis=2, keepdims=True), NEG)
    new = jnp.maximum(old, top)
    shift = jnp.where(live[None], new, -NEG)
    p = jnp.exp2(s - widened(shift, width)).reshape(ROWS, width).astype(jnp.bfloat16)
    factor = jnp.exp2(old - new).reshape(ROWS, HEAD)
    m[half] = new.reshape(ROWS, HEAD)
    update = jnp.dot(p, va[skip:], preferred_element_type=jnp.float32)
    acc[half] = acc[half] * twice(factor) + update


def far_block(base, message, wanted, queries, kt, va, start, count, m, acc):
    @pl.when(wanted & (base + TOK > start))
    def _():
        prepare_block(message, kt, va)

        def body(half, carry):
            whole = (start <= base) & (count >= (half + 1) * HALF)
            short = start >= base + HALF

            @pl.when(whole)
            def _():
                whole_half(half, queries, kt, va, m, acc)

            @pl.when(jnp.logical_not(whole | short))
            def _():
                part_half(half, 0, queries, kt, va, base, start, count, m, acc)

            @pl.when(short)
            def _():
                part_half(half, HALF, queries, kt, va, base, start, count, m, acc)

            return carry

        lax.fori_loop(0, (count + HALF - 1) // HALF, body, 0)


def finish(half, acc, out):
    for h in range(GROUP):
        a = acc[half, h * HALF : (h + 1) * HALF]
        out[half * HALF : (half + 1) * HALF, h * HEAD : (h + 1) * HEAD] = (
            a[:, :HEAD] / a[:, HEAD:]
        ).astype(jnp.bfloat16)


def own_kernel(own, queries, m, acc, kt, va):
    row = id_row(pieces_of(own))
    column = jnp.broadcast_to(row, (HEAD, TOK)).T
    prepare_block(own, kt, va)
    for half in range(2):
        own_half(half, queries, kt, va, column, row, m, acc)


def near_start(ctx, own, sib, r1, r1s):
    mine = pieces_of(own)
    first = mine[:1, :1]
    before = matches(pieces_of(sib), first) * lax.rem(ctx, 2)
    before = before + matches(pieces_of(r1), first) + matches(pieces_of(r1s), first)
    return ctx * TOK - before, matches(mine, first), first


def near_kernel(ctx_ref, own, sib, r1, r1s, queries, m_in, acc_in, m, acc, kt, va):
    ctx = ctx_ref[0]
    odd = lax.rem(ctx, 2) == 1
    start, count, _ = near_start(ctx, own, sib, r1, r1s)
    state = (queries, kt, va, start, count, m, acc)
    far_block((ctx - 1) * TOK, sib, odd, *state)
    far_block((ctx - 1) * TOK, r1s, jnp.logical_not(odd), *state)
    far_block((ctx - 2) * TOK, r1, ctx >= 2, *state)


def last_kernel(
    ctx_ref, own, sib, r1, r1s, r2, r2s, queries, m_in, acc_in, out_hbm, m, acc, kt, va, out, sems
):
    ctx = ctx_ref[0]
    odd = lax.rem(ctx, 2) == 1
    near, count, first = near_start(ctx, own, sib, r1, r1s)
    before = matches(pieces_of(r2), first) + matches(pieces_of(r2s), first)
    start = near - before
    state = (queries, kt, va, start, count, m, acc)
    far_block((ctx - 3) * TOK, r1s, odd & (ctx >= 3), *state)
    far_block((ctx - 3) * TOK, r2s, jnp.logical_not(odd) & (ctx >= 3), *state)
    far_block((ctx - 4) * TOK, r2, ctx >= 4, *state)
    sends = []
    for half in range(2):
        finish(half, acc, out)
        rows = pl.ds(half * HALF, HALF)
        sends.append(pltpu.make_async_copy(out.at[rows], out_hbm.at[rows], sems.at[half]))
        sends[-1].start()
    for send in sends:
        send.wait()


IN_SMEM = pl.BlockSpec(memory_space=pltpu.SMEM)
IN_VMEM = pl.BlockSpec(memory_space=pltpu.VMEM)
IN_HBM = pl.BlockSpec(memory_space=pltpu.HBM)
MESSAGE = jax.ShapeDtypeStruct((TOK + SPARE, 2 * HEAD), jnp.bfloat16)
OUT = jax.ShapeDtypeStruct((TOK, GROUP * HEAD), jnp.bfloat16)
QUERIES = jax.ShapeDtypeStruct((2, ROWS, HEAD), jnp.bfloat16)
TOP = jax.ShapeDtypeStruct((2, ROWS, HEAD), jnp.float32)
ACC = jax.ShapeDtypeStruct((2, ROWS, 2 * HEAD), jnp.float32)
TABLE = pltpu.VMEM((TOK, 2 * HEAD), jnp.float32)
LIMIT = 44 * 2**20
QUERIES_FLOPS = 3 * 10**10


def like(t):
    return pltpu.VMEM(t.shape, t.dtype)


BLOCK = [pltpu.VMEM((HEAD, TOK), jnp.bfloat16), pltpu.VMEM((TOK, 2 * HEAD), jnp.bfloat16)]


def call(kernel, name, ins, outs, scratch, flops, **more):
    specs, types = zip(*outs)
    return pl.pallas_call(
        kernel,
        in_specs=ins,
        out_specs=list(specs),
        out_shape=list(types),
        scratch_shapes=scratch,
        compiler_params=pltpu.CompilerParams(vmem_limit_bytes=LIMIT),
        cost_estimate=pl.CostEstimate(flops=flops, bytes_accessed=2**21, transcendentals=0),
        name=name,
        **more,
    )


def shifted(value, steps):
    return lax.ppermute(value, "ctx", [(i, i + steps) for i in range(N_CTX - steps)])


def swapped(value, senders=(0, 1)):
    return lax.ppermute(value, "ctx", [(i, i ^ 1) for i in range(N_CTX) if i % 2 in senders])


def local(q_proj, key_projection, value_projection, doc_ids):
    table = jnp.asarray(rotary_table())
    ctx = lax.axis_index("ctx").astype(jnp.int32).reshape(1)
    dma = pltpu.SemaphoreType.DMA
    rows = pltpu.VMEM((TOK, HEAD), jnp.bfloat16)
    size = doc_ids.shape[0]
    pieces = jax.ShapeDtypeStruct((KVH, size), jnp.float32)
    (mine,) = call(spread_kernel, "spread", [IN_VMEM], [(IN_VMEM, pieces)], [], 10**6)(doc_ids.reshape(1, size))
    ids = lax.all_to_all(mine, "kvh", 0, 0, tiled=True)
    message, own = call(
        message_kernel,
        "message",
        [IN_SMEM] + [IN_HBM] * 3,
        [(IN_VMEM, MESSAGE)] * 2,
        [rows, rows, TABLE, dma((3,))],
        2 * 10**9,
    )(ctx, key_projection, value_projection, table)
    r1 = shifted(message, 2)

    def with_ids(pieces, message):
        (out,) = call(
            ids_kernel, "ids", [IN_VMEM] * 2, [(IN_VMEM, MESSAGE)], [], 10**6, input_output_aliases={1: 0}
        )(pieces, message)
        return out

    own = with_ids(ids, own)
    ids1 = shifted(ids, 2)
    sib = swapped(own, (0,))
    late, _ = lax.optimization_barrier((ctx, ids))
    (queries,) = call(
        queries_kernel,
        "queries",
        [IN_SMEM] + [IN_HBM] * 2,
        [(IN_VMEM, QUERIES)],
        [like(OUT), TABLE, dma((2,))],
        QUERIES_FLOPS,
    )(late, q_proj, table)
    r1 = with_ids(ids1, r1)
    r2 = shifted(r1, 2)
    r1s = swapped(r1)
    queries, own, r1 = lax.optimization_barrier((queries, own, r1))
    m, acc = call(
        own_kernel, "own", [IN_VMEM] * 2, [(IN_VMEM, TOP), (IN_VMEM, ACC)], BLOCK, 3 * 10**9
    )(own, queries)
    m, acc = call(
        near_kernel,
        "near",
        [IN_SMEM] + [IN_VMEM] * 7,
        [(IN_VMEM, TOP), (IN_VMEM, ACC)],
        BLOCK,
        6 * 10**9,
        input_output_aliases={6: 0, 7: 1},
    )(ctx, own, sib, r1, r1s, queries, m, acc)
    r2, m = lax.optimization_barrier((r2, m))
    r2s = swapped(r2, (1,))
    out, _, _ = call(
        last_kernel,
        "last",
        [IN_SMEM] + [IN_VMEM] * 9,
        [(IN_HBM, OUT), (IN_VMEM, TOP), (IN_VMEM, ACC)],
        BLOCK + [like(OUT), dma((2,))],
        6 * 10**9,
        input_output_aliases={8: 1, 9: 2},
    )(ctx, own, sib, r1, r1s, r2, r2s, queries, m, acc)
    return out


def solution(mesh):
    in_specs = (P("ctx", "kvh"), P("ctx", "kvh"), P("ctx", "kvh"), P(("ctx", "kvh")))
    return jax.shard_map(
        local, mesh=mesh, in_specs=in_specs, out_specs=P("ctx", "kvh"), check_vma=False
    )
```

```python
import functools

import jax
import jax.numpy as jnp
import numpy as np
from jax import lax
from jax.experimental import pallas as pl
from jax.experimental.pallas import tpu as pltpu
from jax.sharding import PartitionSpec as P

HEAD = 128
GROUP = 8
TOK = 512
N_CTX = 32
THETA = 1000000.0
NEG = -1e30
SCALE = float(np.log2(np.e) / np.sqrt(HEAD))
HALF = TOK // 2
ROWS = GROUP * HALF
KVH = 8
SPARE = 16


def rotary_table():
    half = HEAD // 2
    inv = np.float32(THETA) ** (-(np.float32(2.0) * np.arange(half, dtype=np.float32)) / np.float32(HEAD))
    angle = np.arange(N_CTX * TOK, dtype=np.float32)[:, None] * inv.astype(np.float32)[None, :]
    wide = angle.astype(np.float64)
    cosine, sine = np.cos(wide), np.sin(wide)
    table = np.concatenate([cosine, cosine, -sine, sine], axis=1).astype(np.float32)
    return table.reshape(N_CTX, TOK, 2 * HEAD)


def rotate(x, table):
    x = x.astype(jnp.float32)
    return (x * table[:, :HEAD] + pltpu.roll(x, HEAD // 2, 1) * table[:, HEAD:]).astype(jnp.bfloat16)


def message_kernel(ctx_ref, k_hbm, v_hbm, table_hbm, out, k, v, table, sems):
    copies = [
        pltpu.make_async_copy(table_hbm.at[ctx_ref[0]], table, sems.at[0]),
        pltpu.make_async_copy(k_hbm, k, sems.at[1]),
        pltpu.make_async_copy(v_hbm, v, sems.at[2]),
    ]
    for copy in copies:
        copy.start()
    out[TOK:] = jnp.zeros((SPARE, 2 * HEAD), jnp.bfloat16)
    for copy in copies:
        copy.wait()
    out[:TOK, HEAD:] = v[...]
    out[:TOK, :HEAD] = rotate(k[...], table)


def ids_kernel(ids, message_in, message):
    pieces, size = ids.shape
    wide = jnp.concatenate([ids[...], jnp.zeros((pieces, 2 * HEAD - size), jnp.float32)], axis=1)
    wide = jnp.concatenate([wide, jnp.zeros((SPARE - pieces, 2 * HEAD), jnp.float32)], axis=0)
    message[TOK:] = wide.astype(jnp.bfloat16)


def queries_kernel(ctx_ref, q_hbm, table_hbm, queries, raw, table, sems):
    copies = [
        pltpu.make_async_copy(table_hbm.at[ctx_ref[0]], table, sems.at[0]),
        pltpu.make_async_copy(q_hbm, raw, sems.at[1]),
    ]
    for copy in copies:
        copy.start()
    for copy in copies:
        copy.wait()
    for h in range(GROUP):
        turned = rotate(raw[:, h * HEAD : (h + 1) * HEAD], table)
        for half in range(2):
            queries[half, h * HALF : (h + 1) * HALF] = turned[half * HALF : (half + 1) * HALF]


def twice(x):
    return jnp.concatenate([x, x], axis=-1)


def widened(x, width):
    return jnp.concatenate([x] * (width // HEAD), axis=-1)


def pieces_of(message):
    return message[TOK:].astype(jnp.float32)


def id_row(parts):
    size = TOK // KVH
    parts = parts[:KVH]
    lane = lax.broadcasted_iota(jnp.int32, (2 * HEAD, TOK), 1)
    place = (lax.rem(lane, size) == lax.broadcasted_iota(jnp.int32, (2 * HEAD, TOK), 0)).astype(jnp.float32)
    spread = jnp.dot(parts, place, preferred_element_type=jnp.float32)
    mine = lax.broadcasted_iota(jnp.int32, (KVH, TOK), 1) // size
    mine = mine == lax.broadcasted_iota(jnp.int32, (KVH, TOK), 0)
    return jnp.sum(jnp.where(mine, spread, 0.0), axis=0, keepdims=True)


def matches(block, first):
    return jnp.sum(jnp.where(block == first, 1, 0))


def prepare_block(kv, kt, va):
    kt[...] = kv[:TOK, :HEAD].T
    va[:, :HEAD] = kv[:TOK, HEAD:]
    va[:, HEAD:] = jnp.ones((TOK, HEAD), jnp.bfloat16)


def own_half(half, queries, kt, va, column, row, m, acc):
    width = (half + 1) * HALF
    rows = slice(half * HALF, width)
    key = lax.broadcasted_iota(jnp.int32, (HALF, width), 1)
    query = half * HALF + lax.broadcasted_iota(jnp.int32, (HALF, width), 0)
    same = widened(column[rows], width) == row[:, :width]
    bias = jnp.where(same & (key <= query), 0.0, NEG)
    s = jnp.dot(queries[half], kt[:, :width], preferred_element_type=jnp.float32)
    s = s.reshape(GROUP, HALF, width) * SCALE + bias[None]
    top = jnp.broadcast_to(jnp.max(s, axis=2, keepdims=True), (GROUP, HALF, HEAD))
    p = jnp.exp2(s - widened(top, width)).reshape(ROWS, width).astype(jnp.bfloat16)
    m[half] = top.reshape(ROWS, HEAD)
    acc[half] = jnp.dot(p, va[:width], preferred_element_type=jnp.float32)


def whole_half(half, queries, kt, va, m, acc):
    s = jnp.dot(queries[half], kt[...], preferred_element_type=jnp.float32) * SCALE
    old = m[half]
    new = jnp.maximum(old, jnp.max(s, axis=1, keepdims=True))
    p = jnp.exp2(s - widened(new, TOK)).astype(jnp.bfloat16)
    m[half] = new
    update = jnp.dot(p, va[...], preferred_element_type=jnp.float32)
    acc[half] = acc[half] * twice(jnp.exp2(old - new)) + update


def part_half(half, some, skip, queries, kt, va, base, start, count, m, acc):
    width = TOK - skip
    kpos = base + skip + lax.broadcasted_iota(jnp.int32, (1, width), 1)
    key_bias = jnp.where(kpos >= start, 0.0, NEG)
    live = half * HALF + lax.broadcasted_iota(jnp.int32, (some, HEAD), 0) < count

    def heads(ref):
        return ref[half].reshape(GROUP, HALF, ref.shape[-1])[:, :some]

    q = heads(queries).reshape(GROUP * some, HEAD)
    s = jnp.dot(q, kt[:, skip:], preferred_element_type=jnp.float32)
    s = (s * SCALE + key_bias).reshape(GROUP, some, width)
    old = heads(m)
    top = jnp.where(live[None], jnp.max(s, axis=2, keepdims=True), NEG)
    new = jnp.maximum(old, top)
    shift = jnp.where(live[None], new, -NEG)
    p = jnp.exp2(s - widened(shift, width)).reshape(GROUP * some, width).astype(jnp.bfloat16)
    update = jnp.dot(p, va[skip:], preferred_element_type=jnp.float32).reshape(GROUP, some, 2 * HEAD)
    total = heads(acc) * twice(jnp.exp2(old - new)) + update
    for h in range(GROUP):
        m[half, h * HALF : h * HALF + some] = new[h]
        acc[half, h * HALF : h * HALF + some] = total[h]


def far_blocks(blocks, first_base, queries, kt, va, start, count, m, acc):
    for slot, message, wanted in blocks:

        @pl.when(wanted & (first_base - slot * TOK + TOK > start))
        def _():
            prepare_block(message, kt.at[slot], va.at[slot])

    slots = jnp.clip((first_base + 2 * TOK - 1 - start) // TOK, 0, 2)

    def body(i, carry):
        slot, half = i // 2, lax.rem(i, 2)
        base = first_base - slot * TOK
        kt_now, va_now = kt.at[slot], va.at[slot]
        rows = count - half * HALF
        whole = (start <= base) & (rows >= HALF)
        few = rows <= HALF // 2
        part = (rows > 0) & jnp.logical_not(whole)

        @pl.when(whole)
        def _():
            whole_half(half, queries, kt_now, va_now, m, acc)

        for some in (HALF // 2, HALF):
            sized = few if some < HALF else jnp.logical_not(few)
            for skip in (0, HALF):
                short = start >= base + HALF
                chosen = short if skip else jnp.logical_not(short)

                @pl.when(part & sized & chosen)
                def _():
                    part_half(half, some, skip, queries, kt_now, va_now, base, start, count, m, acc)

        return carry

    lax.fori_loop(0, 2 * slots, body, 0)


def finish(half, acc, out):
    for h in range(GROUP):
        a = acc[half, h * HALF : (h + 1) * HALF]
        out[half * HALF : (half + 1) * HALF, h * HEAD : (h + 1) * HEAD] = (
            a[:, :HEAD] / a[:, HEAD:]
        ).astype(jnp.bfloat16)


def own_kernel(own, queries, m, acc, kts, vas):
    kt, va = kts.at[0], vas.at[0]
    row = id_row(pieces_of(own))
    column = jnp.broadcast_to(row, (HEAD, TOK)).T
    prepare_block(own, kt, va)
    for half in range(2):
        own_half(half, queries, kt, va, column, row, m, acc)


def near_start(ctx, own, sib, r1, r1s):
    mine = pieces_of(own)
    first = mine[:1, :1]
    before = matches(pieces_of(sib), first) * lax.rem(ctx, 2)
    before = before + matches(pieces_of(r1), first) + matches(pieces_of(r1s), first)
    return ctx * TOK - before, matches(mine, first), first


def near_kernel(ctx_ref, own, sib, r1, r1s, queries, m_in, acc_in, m, acc, kt, va):
    ctx = ctx_ref[0]
    odd = lax.rem(ctx, 2) == 1
    start, count, _ = near_start(ctx, own, sib, r1, r1s)
    state = (queries, kt, va, start, count, m, acc)
    far_blocks([(0, sib, odd), (0, r1s, jnp.logical_not(odd)), (1, r1, True)], (ctx - 1) * TOK, *state)


def last_kernel(
    ctx_ref, own, sib, r1, r1s, r2, r2s, queries, m_in, acc_in, out_hbm, m, acc, kt, va, out, sems
):
    ctx = ctx_ref[0]
    odd = lax.rem(ctx, 2) == 1
    near, count, first = near_start(ctx, own, sib, r1, r1s)
    before = matches(pieces_of(r2), first) + matches(pieces_of(r2s), first)
    start = near - before
    state = (queries, kt, va, start, count, m, acc)
    far_blocks([(0, r1s, odd), (0, r2s, jnp.logical_not(odd)), (1, r2, True)], (ctx - 3) * TOK, *state)
    sends = []
    for half in range(2):
        finish(half, acc, out)
        rows = pl.ds(half * HALF, HALF)
        sends.append(pltpu.make_async_copy(out.at[rows], out_hbm.at[rows], sems.at[half]))
        sends[-1].start()
    for send in sends:
        send.wait()


IN_SMEM = pl.BlockSpec(memory_space=pltpu.SMEM)
IN_VMEM = pl.BlockSpec(memory_space=pltpu.VMEM)
IN_HBM = pl.BlockSpec(memory_space=pltpu.HBM)
MESSAGE = jax.ShapeDtypeStruct((TOK + SPARE, 2 * HEAD), jnp.bfloat16)
OUT = jax.ShapeDtypeStruct((TOK, GROUP * HEAD), jnp.bfloat16)
QUERIES = jax.ShapeDtypeStruct((2, ROWS, HEAD), jnp.bfloat16)
TOP = jax.ShapeDtypeStruct((2, ROWS, HEAD), jnp.float32)
ACC = jax.ShapeDtypeStruct((2, ROWS, 2 * HEAD), jnp.float32)
TABLE = pltpu.VMEM((TOK, 2 * HEAD), jnp.float32)
LIMIT = 44 * 2**20


def like(t):
    return pltpu.VMEM(t.shape, t.dtype)


BLOCK = [pltpu.VMEM((2, HEAD, TOK), jnp.bfloat16), pltpu.VMEM((2, TOK, 2 * HEAD), jnp.bfloat16)]


def call(kernel, name, ins, outs, scratch, flops, **more):
    specs, types = zip(*outs)
    return pl.pallas_call(
        kernel,
        in_specs=ins,
        out_specs=list(specs),
        out_shape=list(types),
        scratch_shapes=scratch,
        compiler_params=pltpu.CompilerParams(vmem_limit_bytes=LIMIT),
        cost_estimate=pl.CostEstimate(flops=flops, bytes_accessed=2**21, transcendentals=0),
        name=name,
        **more,
    )


def shifted(value, steps):
    return lax.ppermute(value, "ctx", [(i, i + steps) for i in range(N_CTX - steps)])


def swapped(value, senders=(0, 1)):
    return lax.ppermute(value, "ctx", [(i, i ^ 1) for i in range(N_CTX) if i % 2 in senders])


def local(q_proj, key_projection, value_projection, doc_ids):
    table = jnp.asarray(rotary_table())
    ctx = lax.axis_index("ctx").astype(jnp.int32).reshape(1)
    mine = jnp.broadcast_to((doc_ids + 1).astype(jnp.float32), (KVH, doc_ids.shape[0]))
    ids = lax.all_to_all(mine, "kvh", 0, 0, tiled=True)
    dma = pltpu.SemaphoreType.DMA
    rows = pltpu.VMEM((TOK, HEAD), jnp.bfloat16)
    (message,) = call(
        message_kernel,
        "message",
        [IN_SMEM] + [IN_HBM] * 3,
        [(IN_VMEM, MESSAGE)],
        [rows, rows, TABLE, dma((3,))],
        2 * 10**9,
    )(ctx, key_projection, value_projection, table)
    (queries,) = call(
        queries_kernel,
        "queries",
        [IN_SMEM] + [IN_HBM] * 2,
        [(IN_VMEM, QUERIES)],
        [like(OUT), TABLE, dma((2,))],
        2 * 10**9,
    )(ctx, q_proj, table)
    (own,) = call(
        ids_kernel, "ids", [IN_VMEM] * 2, [(IN_VMEM, MESSAGE)], [], 10**6, input_output_aliases={1: 0}
    )(ids, message)
    r1 = shifted(own, 2)
    sib = swapped(own, (0,))
    m, acc = call(
        own_kernel, "own", [IN_VMEM] * 2, [(IN_VMEM, TOP), (IN_VMEM, ACC)], BLOCK, 3 * 10**9
    )(own, queries)
    r1, m = lax.optimization_barrier((r1, m))
    r2 = shifted(r1, 2)
    r1s = swapped(r1)
    m, acc = call(
        near_kernel,
        "near",
        [IN_SMEM] + [IN_VMEM] * 7,
        [(IN_VMEM, TOP), (IN_VMEM, ACC)],
        BLOCK,
        6 * 10**9,
        input_output_aliases={6: 0, 7: 1},
    )(ctx, own, sib, r1, r1s, queries, m, acc)
    r2, m = lax.optimization_barrier((r2, m))
    r2s = swapped(r2, (1,))
    out, _, _ = call(
        last_kernel,
        "last",
        [IN_SMEM] + [IN_VMEM] * 9,
        [(IN_HBM, OUT), (IN_VMEM, TOP), (IN_VMEM, ACC)],
        BLOCK + [like(OUT), dma((2,))],
        6 * 10**9,
        input_output_aliases={8: 1, 9: 2},
    )(ctx, own, sib, r1, r1s, r2, r2s, queries, m, acc)
    return out


def solution(mesh):
    in_specs = (P("ctx", "kvh"), P("ctx", "kvh"), P("ctx", "kvh"), P(("ctx", "kvh")))
    return jax.shard_map(
        local, mesh=mesh, in_specs=in_specs, out_specs=P("ctx", "kvh"), check_vma=False
    )
```
